32 devices in a mesh: expert: 8 (over y, x, core), dp: 4 (over z).
Axes of the slice: x: 2, y: 2, z: 4, core: 2. Of those that a mesh axis runs over, the one named last changes fastest.
Arguments:
- tokens: bfloat16 [32, 200, 768], P(('expert', 'dp')), may hold values from -6 to 6
- cotangent: bfloat16 [32, 200, 768], P(('expert', 'dp')), may hold values from -6 to 6
- image_count: int32 [32], P(('expert', 'dp')), may hold values from 0 to 1, as said below
- expert_ids: int32 [32, 200, 2], P(('expert', 'dp')), may hold values from 0 to 7, all different within a row
- ln1_gain: bfloat16 [768], P('dp'), may hold values from 0.5 to 1.5
- ln1_bias: bfloat16 [768], P('dp'), may hold values from -1 to 1
- qkv_weight: bfloat16 [768, 2304], P('dp'), may hold values from -0.21875 to 0.21875
- qv_bias: bfloat16 [1536], P('dp'), may hold values from -1 to 1
- out_weight: bfloat16 [768, 768], P('dp'), may hold values from -0.625 to 0.625
- out_bias: bfloat16 [768], P('dp'), may hold values from -1 to 1
- ln2_gain: bfloat16 [768], P('dp'), may hold values from 0.5 to 1.5
- ln2_bias: bfloat16 [768], P('dp'), may hold values from -1 to 1
- router_weight: bfloat16 [768, 8], P('dp'), may hold values from -0.125 to 0.125
- expert_w1: bfloat16 [8, 768, 3072], P('expert', 'dp'), may hold values from -0.21875 to 0.21875
- expert_b1: bfloat16 [8, 3072], P('expert', 'dp'), may hold values from -0.59765625 to 0.59765625
- expert_w2: bfloat16 [8, 3072, 768], P('expert', 'dp'), may hold values from -0.875 to 0.875
- expert_b2: bfloat16 [8, 768], P('expert', 'dp'), may hold values from -12 to 12
Outputs:
- mixed: bfloat16 [32, 200, 768], P(('expert', 'dp'))
- tokens_grad: bfloat16 [32, 200, 768], P(('expert', 'dp'))
- ln1_gain_grad: float32 [768], P('dp')
- ln1_bias_grad: float32 [768], P('dp')
- qkv_weight_grad: float32 [768, 2304], P('dp')
- qv_bias_grad: float32 [1536], P('dp')
- out_weight_grad: float32 [768, 768], P('dp')
- out_bias_grad: float32 [768], P('dp')
- ln2_gain_grad: float32 [768], P('dp')
- ln2_bias_grad: float32 [768], P('dp')
- router_weight_grad: float32 [768, 8], P('dp')
- expert_w1_grad: float32 [8, 768, 3072], P('expert', 'dp')
- expert_b1_grad: float32 [8, 3072], P('expert', 'dp')
- expert_w2_grad: float32 [8, 3072, 768], P('expert', 'dp')
- expert_b2_grad: float32 [8, 768], P('expert', 'dp')
The draws below stay inside these ranges and needn't reach their ends.
Inputs may be any that keep to these rules, and one draw needn't show every extreme that they name: Some device holds 1 live images and some other device holds none; a device's first image_count[v] images are live.
All inputs are finite; a program needn't handle non-finite values.
Results may differ from the reference program's by a relative error of at most 0.02.
Values may be sent and summed in bfloat16 or wider, within the bound.
A program may use at most 128 MiB of HBM per device.

```python
from functools import partial
import jax
import jax.numpy as jnp
from jax import lax

D = 768
HEADS = 12
HEAD_DIM = 64
FF = 3072
SEQ = 200
LIVE = 197
IMG_DEV = 1
IMAGES = 32
TOK_DEV = 200
TOKENS = 6400
EXPERTS = 8
CAP = 50
DEVICES = 32


def draw_image_count(key, part):
    key = jax.random.fold_in(key, 7)
    first_key, second_key, third_key, fourth_key = jax.random.split(key, 4)
    partial_counts = jax.random.randint(first_key, (DEVICES,), 0, IMG_DEV)
    shortened = jax.random.randint(fourth_key, (DEVICES,), 0, 4) == 0
    counts = jnp.where(shortened, partial_counts, IMG_DEV)
    full_spot = jax.random.randint(second_key, (), 0, DEVICES)
    empty_spot = (full_spot + 1 + jax.random.randint(third_key, (), 0, DEVICES - 1)) % DEVICES
    device_range = jnp.arange(DEVICES)
    counts = jnp.where(device_range == empty_spot, 0, counts)
    counts = jnp.where(device_range == full_spot, IMG_DEV, counts)
    return counts.astype(jnp.int32)


def levels(key, dims, cuts, smallest, largest):
    factor_of = 1.0
    for dim, parts in cuts:
        steps = jax.random.uniform(jax.random.fold_in(jax.random.fold_in(key, 6), dim), (parts,), jnp.float32, smallest / len(cuts), largest / len(cuts))
        factor_of = factor_of * jnp.repeat(jnp.exp(steps), dims[dim] // parts).reshape((-1,) + (1,) * (len(dims) - 1 - dim))
    return factor_of


def picks_of(stream_key, rows, number_of, top, lift):
    ranking = jax.random.permutation(jax.random.fold_in(stream_key, 1), number_of)
    boost = ranking
    for power in range(3):
        boost = boost * boost // number_of
    boost = boost * lift // number_of
    lots = jax.random.randint(jax.random.fold_in(stream_key, 2), (rows, number_of), 0, 4096) + boost
    fixed_rows = jax.random.permutation(jax.random.fold_in(stream_key, 3), rows)[jnp.arange(number_of) % rows]
    lots = jnp.where(jnp.arange(rows)[:, None] == fixed_rows[None, :], 1 << 14, lots)
    priority = lots * number_of + jnp.arange(number_of)
    return lax.top_k(priority.astype(jnp.int32), top)[1].astype(jnp.int32)


def gaussian(rng, dims, scale, most, shards=(), kind=jnp.bfloat16):
    array = scale * jax.random.normal(rng, dims, jnp.float32)
    if shards:
        array = array * levels(rng, dims, shards, -0.22, 0.18)
    return jnp.clip(array, -most, most).astype(kind)


def setup_inputs(seed: int = 0) -> dict:
    streams_of = jax.random.split(jax.random.key(seed), 18)
    return {
        "tokens": gaussian(streams_of[0], (IMAGES, SEQ, D), 1.0, 6.0, ((0, 32),)),
        "cotangent": gaussian(streams_of[1], (IMAGES, SEQ, D), 1.0, 6.0, ((0, 32),)),
        "image_count": draw_image_count(jax.random.fold_in(streams_of[17], 71), 0),
        "expert_ids": picks_of(streams_of[3], IMAGES * SEQ, EXPERTS, 2, 2048).reshape((IMAGES, SEQ, 2)),
        "ln1_gain": jnp.clip(1.0 + 0.1 * jax.random.normal(streams_of[4], (D,), jnp.float32), 0.5, 1.5).astype(jnp.bfloat16),
        "ln1_bias": gaussian(streams_of[5], (D,), 0.2, 1.0, ((0, 4),)),
        "qkv_weight": gaussian(streams_of[6], (D, 3 * D), D ** -0.5, 0.21875, ((0, 4),)),
        "qv_bias": gaussian(streams_of[7], (2 * D,), 0.2, 1.0, ((0, 4),)),
        "out_weight": gaussian(streams_of[8], (D, D), (D // 8) ** -0.5, 0.625, ((0, 4),)),
        "out_bias": gaussian(streams_of[9], (D,), 0.2, 1.0, ((0, 4),)),
        "ln2_gain": jnp.clip(1.0 + 0.1 * jax.random.normal(streams_of[10], (D,), jnp.float32), 0.5, 1.5).astype(jnp.bfloat16),
        "ln2_bias": gaussian(streams_of[11], (D,), 0.2, 1.0, ((0, 4),)),
        "router_weight": gaussian(streams_of[12], (D, EXPERTS), (3 * D) ** -0.5, 0.125, ((0, 4),)),
        "expert_w1": gaussian(streams_of[13], (EXPERTS, D, FF), D ** -0.5, 0.21875, ((0, 8), (1, 4))),
        "expert_b1": gaussian(streams_of[14], (EXPERTS, FF), 0.1, 0.59765625, ((0, 8), (1, 4))),
        "expert_w2": gaussian(streams_of[15], (EXPERTS, FF, D), (max(1, FF // (EXPERTS * EXPERTS))) ** -0.5, 0.875, ((0, 8), (1, 4))),
        "expert_b2": gaussian(streams_of[16], (EXPERTS, D), 2.0, 12.0, ((0, 8), (1, 4))),
    }


EPSILON = 1e-06
NEGATIVE = -1e+30
PRECISE = lax.Precision.HIGHEST

@jax.custom_vjp
def low(v):
    return lax.optimization_barrier(v.astype(jnp.bfloat16)).astype(jnp.float32)

@jax.custom_vjp
def low_back(v):
    return v

def low_keep(v):
    return (low(v), None)

def low_pass(kept, grad):
    return (grad,)

def back_keep(v):
    return (v, None)

def back_low(kept, grad):
    return (low(grad),)
low.defvjp(low_keep, low_pass)
low_back.defvjp(back_keep, back_low)

def layer_norm(inputs, gain_vec, shift_vec):
    row_mean = lax.optimization_barrier(jnp.mean(inputs, axis=-1, keepdims=True))
    centred = inputs - row_mean
    row_var = lax.optimization_barrier(jnp.mean(centred * centred, axis=-1, keepdims=True))
    return centred * lax.rsqrt(row_var + EPSILON) * gain_vec + shift_vec

def softmax_rows(scores):
    exp_terms = jnp.exp(scores - lax.optimization_barrier(jnp.max(scores, axis=-1, keepdims=True)))
    return exp_terms / lax.optimization_barrier(jnp.sum(exp_terms, axis=-1, keepdims=True))

def attention_part(dense_params, block_in, block_live):
    ln1_gain, ln1_bias, qkv_weight, qv_bias, out_weight, out_bias = dense_params
    normed = low(layer_norm(block_in, ln1_gain, ln1_bias))
    full_bias = jnp.concatenate([qv_bias[:D], jnp.zeros((D,), jnp.float32), qv_bias[D:]])
    projected = jnp.einsum('isd,de->ise', normed, qkv_weight, precision=PRECISE) + full_bias
    projected = low(low_back(projected))
    shaped = projected.reshape(IMG_DEV, SEQ, 3, HEADS, HEAD_DIM)
    queries = shaped[:, :, 0]
    key_vecs = shaped[:, :, 1]
    value_vecs = shaped[:, :, 2]
    scores = jnp.einsum('isha,itha->ihst', queries, key_vecs, precision=PRECISE) * HEAD_DIM ** (-0.5)
    scores = low_back(scores)
    scores = jnp.where(block_live[:, None, None, :], scores, NEGATIVE)
    weights = low(softmax_rows(scores))
    attended = jnp.einsum('ihst,itha->isha', weights, value_vecs, precision=PRECISE)
    attended = low(low_back(attended.reshape(IMG_DEV, SEQ, D)))
    branch = low_back(jnp.einsum('isa,ad->isd', attended, out_weight, precision=PRECISE)) + out_bias
    return block_in + branch

def expert_part(block_pair):
    arrived, w_first, b_first, w_second, b_second = block_pair
    arrived = low_back(arrived)
    hidden_pre = low_back(jnp.dot(arrived, w_first, precision=PRECISE) + b_first)
    activated = low(jax.nn.gelu(hidden_pre, approximate=False))
    return low(low_back(jnp.dot(activated, w_second, precision=PRECISE) + b_second))

def routing(expert_ids, image_count):
    image_index = jnp.arange(IMAGES, dtype=jnp.int32)
    owner_dev = image_index // IMG_DEV
    image_live = image_index % IMG_DEV < image_count[owner_dev]
    token_live = jnp.arange(SEQ, dtype=jnp.int32) < LIVE
    live_mask = image_live[:, None] & token_live[None, :]
    picked = expert_ids.reshape(DEVICES, TOK_DEV * 2)
    live_pairs = jnp.repeat(live_mask.reshape(DEVICES, TOK_DEV), 2, axis=1)
    hot_table = ((picked[:, :, None] == jnp.arange(EXPERTS, dtype=jnp.int32)) & live_pairs[:, :, None]).astype(jnp.int32)
    earlier = jnp.cumsum(hot_table, axis=1) - hot_table
    slot_index = lax.optimization_barrier(jnp.sum(earlier * hot_table, axis=-1))
    kept_pairs = live_pairs & (slot_index < CAP)
    device_index = jnp.arange(DEVICES, dtype=jnp.int32)[:, None]
    position = jnp.where(kept_pairs, picked * (DEVICES * CAP) + device_index * CAP + slot_index, EXPERTS * DEVICES * CAP)
    return (live_mask, position.reshape(TOKENS, 2).astype(jnp.int32), expert_ids.reshape(TOKENS, 2))

def forward(inputs, live_mask, position, picked):
    tokens, ln1_gain, ln1_bias, qkv_weight, qv_bias, out_weight, out_bias, ln2_gain, ln2_bias, router_weight, expert_w1, expert_b1, expert_w2, expert_b2 = inputs
    dense_params = (ln1_gain, ln1_bias, qkv_weight, qv_bias, out_weight, out_bias)
    step_fn = jax.checkpoint(partial(attention_part, dense_params))

    def scan_step(carried, block_pair):
        return (carried, step_fn(block_pair[0], block_pair[1]))
    blocks = tokens.reshape(DEVICES, IMG_DEV, SEQ, D)
    live_blocks = live_mask.reshape(DEVICES, IMG_DEV, SEQ)
    _, after_attn = lax.scan(scan_step, jnp.zeros((), jnp.float32), (blocks, live_blocks))
    after_attn = after_attn.reshape(TOKENS, D)
    normed = low(layer_norm(after_attn, ln2_gain, ln2_bias))
    logits = low_back(jnp.dot(normed, router_weight, precision=PRECISE))
    router_probs = softmax_rows(logits)
    pair_hot = picked[:, :, None] == jnp.arange(EXPERTS, dtype=jnp.int32)
    gate_values = lax.optimization_barrier(jnp.sum(jnp.where(pair_hot, router_probs[:, None, :], 0.0), axis=-1))
    slot_count = EXPERTS * DEVICES * CAP
    pair_index = jnp.arange(TOKENS * 2, dtype=jnp.int32) // 2
    source = jnp.full((slot_count + 1,), TOKENS, jnp.int32).at[position.reshape(-1)].set(pair_index)[:slot_count]
    padded = jnp.concatenate([normed, jnp.zeros((1, D), jnp.float32)])
    arrived = padded[source].reshape(EXPERTS, DEVICES * CAP, D)
    returned = lax.map(jax.checkpoint(expert_part), (arrived, expert_w1, expert_b1, expert_w2, expert_b2))
    back_pad = jnp.concatenate([returned.reshape(slot_count, D), jnp.zeros((1, D), jnp.float32)])
    chosen = back_pad[position]
    final_rows = after_attn + lax.optimization_barrier(jnp.sum(gate_values[:, :, None] * chosen, axis=1))
    return final_rows.reshape(IMAGES, SEQ, D)

def reference(tokens, cotangent, image_count, expert_ids, ln1_gain, ln1_bias, qkv_weight, qv_bias, out_weight, out_bias, ln2_gain, ln2_bias, router_weight, expert_w1, expert_b1, expert_w2, expert_b2):
    live_mask, position, picked = routing(expert_ids, image_count)
    floats = tuple((weight_in.astype(jnp.float32) for weight_in in (tokens, ln1_gain, ln1_bias, qkv_weight, qv_bias, out_weight, out_bias, ln2_gain, ln2_bias, router_weight, expert_w1, expert_b1, expert_w2, expert_b2)))

    def forward_all(*inputs):
        return forward(inputs, live_mask, position, picked)
    result, pullback = jax.vjp(forward_all, *floats)
    cot_masked = cotangent.astype(jnp.float32) * live_mask[:, :, None].astype(jnp.float32)
    gradients = pullback(cot_masked)
    return (result.astype(jnp.bfloat16), gradients[0].astype(jnp.bfloat16), gradients[1], gradients[2], gradients[3], gradients[4], gradients[5], gradients[6], gradients[7], gradients[8], gradients[9], gradients[10], gradients[11], gradients[12], gradients[13])
```

```python
import jax
import jax.numpy as jnp
from jax import lax
from jax.sharding import PartitionSpec as P

HEADS = 12
LIVE = 197


EPSILON = 1e-06
NEGATIVE = -1e30


def layer_norm(inputs, gain_vec, shift_vec):
    row_mean = jnp.mean(inputs, axis=-1, keepdims=True)
    centred = inputs - row_mean
    row_var = jnp.mean(centred * centred, axis=-1, keepdims=True)
    inverse = lax.rsqrt(row_var + EPSILON)
    normal = centred * inverse
    return (normal * gain_vec + shift_vec, normal, inverse)


def norm_back(grad_norm, normal, inverse, gain_vec):
    scaled = grad_norm * gain_vec
    first_mean = jnp.mean(scaled, axis=-1, keepdims=True)
    second = jnp.mean(scaled * normal, axis=-1, keepdims=True)
    return inverse * (scaled - first_mean - normal * second)


def transpose_dot(left_side, right_side):
    return lax.dot_general(
        left_side, right_side, (((0,), (0,)), ((), ())), preferred_element_type=jnp.float32
    )


def dot_transpose(left_side, right_side):
    return lax.dot_general(
        left_side, right_side, (((1,), (1,)), ((), ())), preferred_element_type=jnp.float32
    )


def shards(
    tokens,
    cotangent,
    image_count,
    expert_ids,
    ln1_gain,
    ln1_bias,
    qkv_weight,
    qv_bias,
    out_weight,
    out_bias,
    ln2_gain,
    ln2_bias,
    router_weight,
    expert_w1,
    expert_b1,
    expert_w2,
    expert_b2,
):
    both = ("expert", "dp")
    img_count, seq_len, model_width = tokens.shape
    tok_rows = img_count * seq_len
    expert_count = router_weight.shape[1]
    dp_count = lax.axis_size("dp")
    dp_index = lax.axis_index("dp")
    capacity = max(2, (2 * LIVE * img_count + expert_count - 1) // expert_count)
    slot_rows = -(-(capacity + 3) // 8) * 8
    slot_count = expert_count * slot_rows
    head_count = HEADS
    head_size = model_width // head_count
    scale_factor = head_size ** (-0.5)
    owned = model_width // dp_count
    f32 = jnp.float32
    bf16 = jnp.bfloat16

    small_in = (ln1_gain, ln1_bias, qv_bias, out_bias, ln2_gain, ln2_bias, router_weight)
    small_sizes = [part.size for part in small_in]
    packed_small = jnp.concatenate([part.reshape(-1) for part in small_in])
    small_full = lax.all_gather(packed_small, "dp", axis=0, tiled=False)
    qkv_full = lax.all_gather(qkv_weight, "dp", axis=0, tiled=True)
    out_full = lax.all_gather(out_weight, "dp", axis=0, tiled=True)
    cuts = [sum(small_sizes[:i]) for i in range(len(small_sizes) + 1)]
    gain_one, shift_one, qv_float, out_shift, gain_two, shift_two = (
        small_full[:, cuts[i] : cuts[i + 1]].reshape(-1).astype(f32) for i in range(6)
    )
    router_full = small_full[:, cuts[6] : cuts[7]].reshape(model_width, expert_count)

    image_live = jnp.arange(img_count) < image_count[0]
    token_live = jnp.arange(seq_len) < LIVE
    live_mask = image_live[:, None] & token_live[None, :]
    live_rows = live_mask.reshape(tok_rows)
    key_live = live_mask[:, None, None, :]
    picked = expert_ids.reshape(tok_rows, 2)
    expert_range = jnp.arange(expert_count, dtype=jnp.int32)
    pair_hot = picked[:, :, None] == expert_range
    live_hot = jnp.where(live_rows[:, None, None], pair_hot, False)
    both_hot = jnp.sum(live_hot.astype(bf16), axis=1)
    row_range = jnp.arange(tok_rows)
    below = (row_range[:, None] > row_range[None, :]).astype(bf16)
    earlier = jnp.dot(below, both_hot, preferred_element_type=f32)
    slot_one = jnp.sum(jnp.where(live_hot[:, 0], earlier, 0.0), axis=-1)
    slot_two = jnp.sum(jnp.where(live_hot[:, 1], earlier, 0.0), axis=-1)
    slot_range = jnp.arange(slot_count, dtype=jnp.int32)

    def place(slot, choice):
        slot = slot.astype(jnp.int32)
        kept = live_rows & (slot < capacity)
        return jnp.where(kept, picked[:, choice] * slot_rows + slot, -1)

    position_one = place(slot_one, 0)
    position_two = place(slot_two, 1)
    hot_one = (position_one[:, None] == slot_range).astype(bf16)
    hot_two = (position_two[:, None] == slot_range).astype(bf16)
    hot_both = hot_one + hot_two

    def spread(chunks):
        wide = jnp.broadcast_to(
            chunks.reshape(expert_count, 1, slot_rows, model_width),
            (expert_count, dp_count, slot_rows, model_width),
        ).reshape(expert_count * dp_count, slot_rows, model_width)
        return lax.all_to_all(wide, both, split_axis=0, concat_axis=0, tiled=True)

    def gather_back(partial_rows):
        returned = lax.all_to_all(
            partial_rows.reshape(expert_count * dp_count, slot_rows, model_width),
            both,
            split_axis=0,
            concat_axis=0,
            tiled=True,
        )
        returned = returned.reshape(expert_count, dp_count, slot_rows, model_width)
        return jnp.sum(returned.astype(f32), axis=1).astype(bf16).reshape(slot_count, model_width)

    cot_rows = cotangent.reshape(tok_rows, model_width)
    cot_arrived = spread(transpose_dot(hot_both, cot_rows).astype(bf16))
    w_first = lax.all_to_all(expert_w1[0], "dp", split_axis=1, concat_axis=0, tiled=True)
    b_first = expert_b1[0].astype(f32)
    w_second = expert_w2[0]
    b_second = lax.dynamic_update_slice(
        jnp.zeros((model_width,), f32), expert_b2[0].astype(f32), (dp_index * owned,)
    )

    inputs = tokens.reshape(tok_rows, model_width).astype(f32)
    normed_one, normal_one, inverse_one = layer_norm(inputs, gain_one, shift_one)
    normed_one = normed_one.astype(bf16)
    full_bias = jnp.concatenate(
        [qv_float[:model_width], jnp.zeros((model_width,), f32), qv_float[model_width:]]
    )
    projected = (jnp.dot(normed_one, qkv_full, preferred_element_type=f32) + full_bias).astype(bf16)
    shaped = projected.reshape(img_count, seq_len, 3, head_count, head_size)
    queries = shaped[:, :, 0]
    key_vecs = shaped[:, :, 1]
    value_vecs = shaped[:, :, 2]
    scores = (
        jnp.einsum("isha,itha->ihst", queries, key_vecs, preferred_element_type=f32) * scale_factor
    )
    scores = jnp.where(key_live, scores, NEGATIVE)
    row_max = jnp.max(scores, axis=-1, keepdims=True)
    exp_terms = jnp.exp(scores - row_max)
    row_total = jnp.sum(exp_terms, axis=-1, keepdims=True)
    prob_attn = exp_terms / row_total
    weights = prob_attn.astype(bf16)
    attended = jnp.einsum("ihst,itha->isha", weights, value_vecs, preferred_element_type=f32)
    attended = attended.reshape(tok_rows, model_width).astype(bf16)
    after_attn = inputs + jnp.dot(attended, out_full, preferred_element_type=f32) + out_shift
    normed_two, normal_two, inverse_two = layer_norm(after_attn, gain_two, shift_two)
    normed_two = normed_two.astype(bf16)

    logits = jnp.dot(normed_two, router_full, preferred_element_type=f32)
    logit_exp = jnp.exp(logits - jnp.max(logits, axis=-1, keepdims=True))
    router_probs = logit_exp / jnp.sum(logit_exp, axis=-1, keepdims=True)
    gate_one = jnp.sum(jnp.where(pair_hot[:, 0], router_probs, 0.0), axis=-1)
    gate_two = jnp.sum(jnp.where(pair_hot[:, 1], router_probs, 0.0), axis=-1)

    slot_gate = jnp.sum(
        hot_one.astype(f32) * gate_one[:, None] + hot_two.astype(f32) * gate_two[:, None], axis=0
    )
    gate_high = lax.reduce_precision(slot_gate, 8, 7)
    gate_mid = lax.reduce_precision(slot_gate - gate_high, 8, 7)
    gate_low = slot_gate - gate_high - gate_mid
    gate_parts = jnp.stack([gate_high, gate_mid, gate_low]).astype(bf16)
    gate_parts = gate_parts.reshape(3, expert_count, slot_rows).transpose(1, 0, 2)
    gate_block = jnp.pad(
        gate_parts,
        ((0, 0), (capacity, slot_rows - capacity - 3), (0, model_width - slot_rows)),
    )
    send_rows = transpose_dot(hot_both, normed_two).astype(bf16)
    send_rows = send_rows.reshape(expert_count, slot_rows, model_width) + gate_block
    arrived = spread(send_rows)
    in_gather = lax.all_gather(
        jnp.concatenate([normed_one, attended], axis=1), "expert", axis=0, tiled=True
    )

    gates_in = jnp.sum(
        arrived[:, capacity : capacity + 3, :slot_rows].astype(f32), axis=1, keepdims=False
    )
    flat_in = arrived.reshape(-1, model_width)
    flat_grad = (gates_in[:, :, None] * cot_arrived.astype(f32)).astype(bf16)
    flat_grad = flat_grad.reshape(-1, model_width)
    hidden_pre = jnp.dot(flat_in, w_first, preferred_element_type=f32) + b_first
    normal_cdf = 0.5 * (1.0 + lax.erf(hidden_pre * (0.5**0.5)))
    activated = (hidden_pre * normal_cdf).astype(bf16)
    slope = normal_cdf + hidden_pre * jnp.exp(-0.5 * hidden_pre * hidden_pre) * (
        0.3989422804014327
    )
    produced = (jnp.dot(activated, w_second, preferred_element_type=f32) + b_second).astype(bf16)
    returned = gather_back(produced)
    grad_pre = (dot_transpose(flat_grad, w_second) * slope).astype(bf16)
    grad_input = dot_transpose(grad_pre, w_first).astype(bf16)
    sent_back = gather_back(grad_input)
    grad_w1 = transpose_dot(flat_in, grad_pre).astype(bf16)
    grad_w1 = lax.all_to_all(grad_w1, "dp", split_axis=0, concat_axis=1, tiled=True)
    grad_w1 = grad_w1.astype(f32)[None]
    grad_b1 = jnp.sum(grad_pre, axis=0, dtype=f32)[None]
    grad_w2 = transpose_dot(activated, flat_grad)[None]
    grad_b2 = jnp.sum(flat_grad, axis=0, dtype=f32)
    grad_b2 = lax.dynamic_slice(grad_b2, (dp_index * owned,), (owned,))[None]

    chosen_one = jnp.dot(hot_one, returned, preferred_element_type=f32)
    chosen_two = jnp.dot(hot_two, returned, preferred_element_type=f32)
    final_rows = after_attn + (gate_one[:, None] * chosen_one + gate_two[:, None] * chosen_two)
    mixed_out = final_rows.astype(bf16).reshape(tokens.shape)
    grad_out = jnp.where(live_rows[:, None], cot_rows.astype(f32), 0.0)
    grad_gate_one = jnp.sum(grad_out * chosen_one, axis=-1, keepdims=True)
    grad_gate_two = jnp.sum(grad_out * chosen_two, axis=-1, keepdims=True)
    grad_probs = jnp.where(pair_hot[:, 0], grad_gate_one, 0.0) + jnp.where(
        pair_hot[:, 1], grad_gate_two, 0.0
    )
    grad_logits = router_probs * (
        grad_probs - jnp.sum(router_probs * grad_probs, axis=-1, keepdims=True)
    )
    grad_logits = grad_logits.astype(bf16)
    grad_router = transpose_dot(normed_two, grad_logits)
    grad_normed = jnp.dot(hot_both, sent_back, preferred_element_type=f32)
    grad_normed = grad_normed + dot_transpose(grad_logits, router_full)
    grad_gain_two = jnp.sum(grad_normed * normal_two, axis=0)
    grad_shift_two = jnp.sum(grad_normed, axis=0)
    grad_after = grad_out + norm_back(grad_normed, normal_two, inverse_two, gain_two)
    grad_out_shift = jnp.sum(grad_after, axis=0)
    grad_branch = grad_after.astype(bf16)
    grad_attended = (
        dot_transpose(grad_branch, out_full)
        .astype(bf16)
        .reshape(img_count, seq_len, head_count, head_size)
    )
    grad_weights = jnp.einsum(
        "isha,itha->ihst", grad_attended, value_vecs, preferred_element_type=f32
    )
    row_dot = jnp.sum(prob_attn * grad_weights, axis=-1, keepdims=True)
    grad_scores = jnp.where(key_live, prob_attn * (grad_weights - row_dot), 0.0).astype(bf16)
    grad_queries = (
        jnp.einsum("ihst,itha->isha", grad_scores, key_vecs, preferred_element_type=f32)
        * scale_factor
    )
    grad_keys = (
        jnp.einsum("ihst,isha->itha", grad_scores, queries, preferred_element_type=f32)
        * scale_factor
    )
    grad_values = jnp.einsum("ihst,isha->itha", weights, grad_attended, preferred_element_type=f32)
    grad_projected = (
        jnp.stack([grad_queries, grad_keys, grad_values], axis=2)
        .reshape(tok_rows, 3 * model_width)
        .astype(bf16)
    )
    column_sums = jnp.sum(grad_projected, axis=0, dtype=f32)
    grad_qv = jnp.concatenate([column_sums[:model_width], column_sums[2 * model_width :]])
    grad_normed_one = dot_transpose(grad_projected, qkv_full)
    grad_gain_one = jnp.sum(grad_normed_one * normal_one, axis=0)
    grad_shift_one = jnp.sum(grad_normed_one, axis=0)
    grad_inputs = grad_after + norm_back(grad_normed_one, normal_one, inverse_one, gain_one)
    tokens_grad = grad_inputs.astype(bf16).reshape(tokens.shape)

    small_grads = (
        grad_gain_one,
        grad_shift_one,
        grad_qv,
        grad_out_shift,
        grad_gain_two,
        grad_shift_two,
        grad_router,
    )
    small_pack = jnp.concatenate([part.reshape(dp_count, -1) for part in small_grads], axis=1)
    qkv_part = 3 * model_width // expert_count
    out_part = model_width // expert_count
    share = qkv_part + out_part
    extra = -(-small_pack.shape[1] // (expert_count * share))
    small_pack = jnp.pad(
        small_pack, ((0, 0), (0, expert_count * share * extra - small_pack.shape[1]))
    )
    small_pack = (
        small_pack.astype(bf16)
        .reshape(dp_count, expert_count, extra, share)
        .transpose(1, 0, 2, 3)
        .reshape(expert_count, dp_count * extra, share)
    )
    column_share = jnp.concatenate(
        [
            grad_projected.reshape(tok_rows, expert_count, qkv_part),
            grad_branch.reshape(tok_rows, expert_count, out_part),
        ],
        axis=2,
    ).transpose(1, 0, 2)
    shares_in = lax.all_to_all(
        jnp.concatenate([column_share, small_pack], axis=1),
        "expert",
        split_axis=0,
        concat_axis=0,
        tiled=True,
    )
    token_share = shares_in[:, :tok_rows].reshape(expert_count * tok_rows, share)
    small_share = jnp.sum(shares_in[:, tok_rows:].astype(f32), axis=0)
    qkv_rows = transpose_dot(in_gather[:, :model_width], token_share[:, :qkv_part])
    out_rows = transpose_dot(in_gather[:, model_width:], token_share[:, qkv_part:])
    partial_grad = jnp.concatenate(
        [
            jnp.concatenate([qkv_rows, out_rows], axis=1).reshape(dp_count, owned, share),
            small_share.reshape(dp_count, extra, share),
        ],
        axis=1,
    ).astype(bf16)
    summed = lax.all_to_all(partial_grad, "dp", split_axis=0, concat_axis=0, tiled=True)
    summed = jnp.sum(summed.astype(f32), axis=0).astype(bf16)
    everyone = lax.all_to_all(
        jnp.broadcast_to(summed[None], (expert_count,) + summed.shape),
        "expert",
        split_axis=0,
        concat_axis=0,
        tiled=True,
    ).astype(f32)
    qkv_total = everyone[:, :owned, :qkv_part].transpose(1, 0, 2).reshape(owned, 3 * model_width)
    out_total = everyone[:, :owned, qkv_part:].transpose(1, 0, 2).reshape(owned, model_width)
    small_total = everyone[:, owned:].reshape(-1)
    (
        gain_one_total,
        shift_one_total,
        qv_total,
        out_shift_total,
        gain_two_total,
        shift_two_total,
        router_total,
    ) = (
        small_total[cuts[i] : cuts[i + 1]].reshape(small_in[i].shape) for i in range(7)
    )
    return (
        mixed_out,
        tokens_grad,
        gain_one_total,
        shift_one_total,
        qkv_total,
        qv_total,
        out_total,
        out_shift_total,
        gain_two_total,
        shift_two_total,
        router_total,
        grad_w1,
        grad_b1,
        grad_w2,
        grad_b2,
    )


def solution(mesh):
    in_specs = (
        P(("expert", "dp"), None, None),
        P(("expert", "dp"), None, None),
        P(("expert", "dp")),
        P(("expert", "dp"), None, None),
        P("dp"),
        P("dp"),
        P("dp", None),
        P("dp"),
        P("dp", None),
        P("dp"),
        P("dp"),
        P("dp"),
        P("dp", None),
        P("expert", "dp", None),
        P("expert", "dp"),
        P("expert", "dp", None),
        P("expert", "dp"),
    )
    out_specs = (
        P(("expert", "dp"), None, None),
        P(("expert", "dp"), None, None),
        P("dp"),
        P("dp"),
        P("dp", None),
        P("dp"),
        P("dp", None),
        P("dp"),
        P("dp"),
        P("dp"),
        P("dp", None),
        P("expert", "dp", None),
        P("expert", "dp"),
        P("expert", "dp", None),
        P("expert", "dp"),
    )
    return jax.shard_map(shards, mesh=mesh, in_specs=in_specs, out_specs=out_specs, check_vma=False)
```

```python
import functools

import jax
import jax.numpy as jnp
from jax import lax
from jax.experimental import pallas as pl
from jax.experimental.pallas import tpu as pltpu
from jax.sharding import PartitionSpec as P

HEADS = 12
LIVE = 197


EPSILON = 1e-06
NEGATIVE = -1e30


def layer_norm(inputs, gain_vec, shift_vec):
    row_mean = jnp.mean(inputs, axis=-1, keepdims=True)
    centred = inputs - row_mean
    row_var = jnp.mean(centred * centred, axis=-1, keepdims=True)
    inverse = lax.rsqrt(row_var + EPSILON)
    normal = centred * inverse
    return (normal * gain_vec + shift_vec, normal, inverse)


def norm_back(grad_norm, normal, inverse, gain_vec):
    scaled = grad_norm * gain_vec
    first_mean = jnp.mean(scaled, axis=-1, keepdims=True)
    second = jnp.mean(scaled * normal, axis=-1, keepdims=True)
    return inverse * (scaled - first_mean - normal * second)


def transpose_dot(left_side, right_side):
    return lax.dot_general(
        left_side, right_side, (((0,), (0,)), ((), ())), preferred_element_type=jnp.float32
    )


def dot_transpose(left_side, right_side):
    return lax.dot_general(
        left_side, right_side, (((1,), (1,)), ((), ())), preferred_element_type=jnp.float32
    )

MESH = pl.DeviceIdType.MESH
SMALL_ROWS = 16


def gather_kernel(planes, dp_count, piece, small, full, small_full, loc, ss, rs, sz, rz, sc, rc, sx, rx):
    expert = lax.axis_index("expert")
    depth = lax.axis_index("dp")
    expert_total = 2 * planes
    rows, columns = piece.shape
    mate = expert + 1 - 2 * lax.rem(expert, 2)

    def chip(offset):
        return lax.rem(expert + 2 * offset, expert_total)

    def layer(offset):
        return lax.rem(depth + offset, dp_count)

    def region(m, k):
        column = lax.rem(expert - 2 * m + expert_total, expert_total)
        row = lax.rem(depth - k + dp_count, dp_count)
        return full.at[
            pl.ds(pl.multiple_of(row * rows, 16), rows),
            pl.ds(pl.multiple_of(column * columns, 128), columns),
        ]

    def mate_region(m, k):
        column = lax.rem(mate - 2 * m + expert_total, expert_total)
        row = lax.rem(depth - k + dp_count, dp_count)
        return full.at[
            pl.ds(pl.multiple_of(row * rows, 16), rows),
            pl.ds(pl.multiple_of(column * columns, 128), columns),
        ]

    barrier = pltpu.get_barrier_semaphore()
    for k in range(1, dp_count):
        pl.semaphore_signal(barrier, inc=1, device_id=(expert, layer(k)), device_id_type=MESH)
    for m in range(1, planes):
        pl.semaphore_signal(barrier, inc=1, device_id=(chip(m), depth), device_id_type=MESH)
    pl.semaphore_signal(barrier, inc=1, device_id=(mate, depth), device_id_type=MESH)
    own = pltpu.make_async_copy(piece, region(0, 0), loc.at[0])
    own.start()
    own_small = pltpu.make_async_copy(small, small_full.at[depth], loc.at[1])
    own_small.start()
    pl.semaphore_wait(barrier, dp_count + planes - 1)

    def remote(src, dst, send, recv, device):
        return pltpu.make_async_remote_copy(
            src_ref=src, dst_ref=dst, send_sem=send, recv_sem=recv, device_id=device, device_id_type=MESH
        )

    sent = []

    def start(*what):
        copy = remote(*what)
        copy.start()
        sent.append(copy)

    for k in range(1, dp_count):
        start(small, small_full.at[depth], ss.at[k], rs.at[k], (expert, layer(k)))
        start(piece, region(0, 0), sz.at[k], rz.at[k], (expert, layer(k)))
    for k in range(dp_count):
        if k == 0:
            src = piece
        else:
            src = region(0, k)
            remote(src, src, sz.at[k], rz.at[k], (expert, layer(k))).wait_recv()
        for m in range(1, planes):
            slot = m * dp_count + k
            start(src, region(0, k), sc.at[slot], rc.at[slot], (chip(m), depth))
        start(src, region(0, k), sx.at[k], rx.at[k], (mate, depth))
    for k in range(dp_count):
        for m in range(1, planes):
            slot = m * dp_count + k
            here = region(m, k)
            remote(here, here, sc.at[slot], rc.at[slot], (chip(m), depth)).wait_recv()
            start(here, here, sx.at[slot], rx.at[slot], (mate, depth))
    for k in range(1, dp_count):
        there = small_full.at[lax.rem(depth - k + dp_count, dp_count)]
        remote(there, there, ss.at[k], rs.at[k], (expert, layer(k))).wait_recv()
    for k in range(dp_count):
        for m in range(planes):
            slot = m * dp_count + k
            here = mate_region(m, k)
            remote(here, here, sx.at[slot], rx.at[slot], (mate, depth)).wait_recv()
    for copy in sent:
        copy.wait_send()
    own.wait()
    own_small.wait()


def gather_pieces(piece, small, expert_count, dp_count):
    planes = expert_count // 2
    rows, columns = piece.shape
    dma = pltpu.SemaphoreType.DMA
    return pl.pallas_call(
        functools.partial(gather_kernel, planes, dp_count),
        out_shape=(
            jax.ShapeDtypeStruct((dp_count * rows, expert_count * columns), piece.dtype),
            jax.ShapeDtypeStruct((dp_count,) + small.shape, small.dtype),
        ),
        in_specs=[pl.BlockSpec(memory_space=pl.ANY)] * 2,
        out_specs=[pl.BlockSpec(memory_space=pl.ANY)] * 2,
        scratch_shapes=[dma((2,))]
        + [dma((dp_count,))] * 4
        + [dma((planes * dp_count,))] * 4,
        compiler_params=pltpu.CompilerParams(collective_id=0, has_side_effects=True),
    )(piece, small)


def shards(
    tokens,
    cotangent,
    image_count,
    expert_ids,
    ln1_gain,
    ln1_bias,
    qkv_weight,
    qv_bias,
    out_weight,
    out_bias,
    ln2_gain,
    ln2_bias,
    router_weight,
    expert_w1,
    expert_b1,
    expert_w2,
    expert_b2,
):
    both = ("expert", "dp")
    img_count, seq_len, model_width = tokens.shape
    tok_rows = img_count * seq_len
    expert_count = router_weight.shape[1]
    dp_count = lax.axis_size("dp")
    dp_index = lax.axis_index("dp")
    capacity = max(2, (2 * LIVE * img_count + expert_count - 1) // expert_count)
    slot_rows = -(-(capacity + 3) // 8) * 8
    slot_count = expert_count * slot_rows
    head_count = HEADS
    head_size = model_width // head_count
    scale_factor = head_size ** (-0.5)
    owned = model_width // dp_count
    f32 = jnp.float32
    bf16 = jnp.bfloat16

    small_in = (ln1_gain, ln1_bias, qv_bias, out_bias, ln2_gain, ln2_bias, router_weight)
    small_sizes = [part.size for part in small_in]
    packed_small = jnp.concatenate([part.reshape(-1) for part in small_in])
    width = 4 * model_width // expert_count
    if width % 128 == 0 and owned % 16 == 0:
        joined = jnp.concatenate([qkv_weight, out_weight], axis=1)
        piece = lax.dynamic_slice(
            joined, (0, lax.axis_index("expert") * width), (owned, width)
        )
        small_wide = -(-packed_small.size // (SMALL_ROWS * 128)) * 128
        packed_small = jnp.pad(packed_small, (0, SMALL_ROWS * small_wide - packed_small.size))
        full, small_full = gather_pieces(
            piece, packed_small.reshape(SMALL_ROWS, small_wide), expert_count, dp_count
        )
        small_full = small_full.reshape(dp_count, -1)
        qkv_full = full[:, : 3 * model_width]
        out_full = full[:, 3 * model_width :]
    else:
        small_full = lax.all_gather(packed_small, "dp", axis=0, tiled=False)
        qkv_full = lax.all_gather(qkv_weight, "dp", axis=0, tiled=True)
        out_full = lax.all_gather(out_weight, "dp", axis=0, tiled=True)
    cuts = [sum(small_sizes[:i]) for i in range(len(small_sizes) + 1)]
    gain_one, shift_one, qv_float, out_shift, gain_two, shift_two = (
        small_full[:, cuts[i] : cuts[i + 1]].reshape(-1).astype(f32) for i in range(6)
    )
    router_full = small_full[:, cuts[6] : cuts[7]].reshape(model_width, expert_count)

    image_live = jnp.arange(img_count) < image_count[0]
    token_live = jnp.arange(seq_len) < LIVE
    live_mask = image_live[:, None] & token_live[None, :]
    live_rows = live_mask.reshape(tok_rows)
    key_live = live_mask[:, None, None, :]
    picked = expert_ids.reshape(tok_rows, 2)
    expert_range = jnp.arange(expert_count, dtype=jnp.int32)
    pair_hot = picked[:, :, None] == expert_range
    live_hot = jnp.where(live_rows[:, None, None], pair_hot, False)
    both_hot = jnp.sum(live_hot.astype(bf16), axis=1)
    row_range = jnp.arange(tok_rows)
    below = (row_range[:, None] > row_range[None, :]).astype(bf16)
    earlier = jnp.dot(below, both_hot, preferred_element_type=f32)
    slot_one = jnp.sum(jnp.where(live_hot[:, 0], earlier, 0.0), axis=-1)
    slot_two = jnp.sum(jnp.where(live_hot[:, 1], earlier, 0.0), axis=-1)
    slot_range = jnp.arange(slot_count, dtype=jnp.int32)

    def place(slot, choice):
        slot = slot.astype(jnp.int32)
        kept = live_rows & (slot < capacity)
        return jnp.where(kept, picked[:, choice] * slot_rows + slot, -1)

    position_one = place(slot_one, 0)
    position_two = place(slot_two, 1)
    hot_one = (position_one[:, None] == slot_range).astype(bf16)
    hot_two = (position_two[:, None] == slot_range).astype(bf16)
    hot_both = hot_one + hot_two

    def spread(chunks):
        wide = jnp.broadcast_to(
            chunks.reshape(expert_count, 1, slot_rows, model_width),
            (expert_count, dp_count, slot_rows, model_width),
        ).reshape(expert_count * dp_count, slot_rows, model_width)
        return lax.all_to_all(wide, both, split_axis=0, concat_axis=0, tiled=True)

    def gather_back(partial_rows):
        returned = lax.all_to_all(
            partial_rows.reshape(expert_count * dp_count, slot_rows, model_width),
            both,
            split_axis=0,
            concat_axis=0,
            tiled=True,
        )
        returned = returned.reshape(expert_count, dp_count, slot_rows, model_width)
        return jnp.sum(returned.astype(f32), axis=1).astype(bf16).reshape(slot_count, model_width)

    cot_rows = cotangent.reshape(tok_rows, model_width)
    cot_arrived = spread(transpose_dot(hot_both, cot_rows).astype(bf16))
    w_first = lax.all_to_all(expert_w1[0], "dp", split_axis=1, concat_axis=0, tiled=True)
    b_first = expert_b1[0].astype(f32)
    w_second = expert_w2[0]
    b_second = lax.dynamic_update_slice(
        jnp.zeros((model_width,), f32), expert_b2[0].astype(f32), (dp_index * owned,)
    )

    inputs = tokens.reshape(tok_rows, model_width).astype(f32)
    normed_one, normal_one, inverse_one = layer_norm(inputs, gain_one, shift_one)
    normed_one = normed_one.astype(bf16)
    full_bias = jnp.concatenate(
        [qv_float[:model_width], jnp.zeros((model_width,), f32), qv_float[model_width:]]
    )
    projected = (jnp.dot(normed_one, qkv_full, preferred_element_type=f32) + full_bias).astype(bf16)
    shaped = projected.reshape(img_count, seq_len, 3, head_count, head_size)
    queries = shaped[:, :, 0]
    key_vecs = shaped[:, :, 1]
    value_vecs = shaped[:, :, 2]
    scores = (
        jnp.einsum("isha,itha->ihst", queries, key_vecs, preferred_element_type=f32) * scale_factor
    )
    scores = jnp.where(key_live, scores, NEGATIVE)
    row_max = jnp.max(scores, axis=-1, keepdims=True)
    exp_terms = jnp.exp(scores - row_max)
    row_total = jnp.sum(exp_terms, axis=-1, keepdims=True)
    prob_attn = exp_terms / row_total
    weights = prob_attn.astype(bf16)
    attended = jnp.einsum("ihst,itha->isha", weights, value_vecs, preferred_element_type=f32)
    attended = attended.reshape(tok_rows, model_width).astype(bf16)
    attended, cot_arrived, w_first = lax.optimization_barrier((attended, cot_arrived, w_first))
    after_attn = inputs + jnp.dot(attended, out_full, preferred_element_type=f32) + out_shift
    normed_two, normal_two, inverse_two = layer_norm(after_attn, gain_two, shift_two)
    normed_two = normed_two.astype(bf16)

    logits = jnp.dot(normed_two, router_full, preferred_element_type=f32)
    logit_exp = jnp.exp(logits - jnp.max(logits, axis=-1, keepdims=True))
    router_probs = logit_exp / jnp.sum(logit_exp, axis=-1, keepdims=True)
    gate_one = jnp.sum(jnp.where(pair_hot[:, 0], router_probs, 0.0), axis=-1)
    gate_two = jnp.sum(jnp.where(pair_hot[:, 1], router_probs, 0.0), axis=-1)

    slot_gate = jnp.sum(
        hot_one.astype(f32) * gate_one[:, None] + hot_two.astype(f32) * gate_two[:, None], axis=0
    )
    gate_high = lax.reduce_precision(slot_gate, 8, 7)
    gate_mid = lax.reduce_precision(slot_gate - gate_high, 8, 7)
    gate_low = slot_gate - gate_high - gate_mid
    gate_parts = jnp.stack([gate_high, gate_mid, gate_low]).astype(bf16)
    gate_parts = gate_parts.reshape(3, expert_count, slot_rows).transpose(1, 0, 2)
    gate_block = jnp.pad(
        gate_parts,
        ((0, 0), (capacity, slot_rows - capacity - 3), (0, model_width - slot_rows)),
    )
    send_rows = transpose_dot(hot_both, normed_two).astype(bf16)
    send_rows = send_rows.reshape(expert_count, slot_rows, model_width) + gate_block
    arrived = spread(send_rows)
    in_gather = lax.all_gather(
        jnp.concatenate([normed_one, attended], axis=1), "expert", axis=0, tiled=True
    )

    gates_in = jnp.sum(
        arrived[:, capacity : capacity + 3, :slot_rows].astype(f32), axis=1, keepdims=False
    )
    flat_in = arrived.reshape(-1, model_width)
    flat_grad = (gates_in[:, :, None] * cot_arrived.astype(f32)).astype(bf16)
    flat_grad = flat_grad.reshape(-1, model_width)
    hidden_pre = jnp.dot(flat_in, w_first, preferred_element_type=f32) + b_first
    normal_cdf = 0.5 * (1.0 + lax.erf(hidden_pre * (0.5**0.5)))
    activated = (hidden_pre * normal_cdf).astype(bf16)
    slope = normal_cdf + hidden_pre * jnp.exp(-0.5 * hidden_pre * hidden_pre) * (
        0.3989422804014327
    )
    produced = (jnp.dot(activated, w_second, preferred_element_type=f32) + b_second).astype(bf16)
    returned = gather_back(produced)
    grad_pre = (dot_transpose(flat_grad, w_second) * slope).astype(bf16)
    grad_input = dot_transpose(grad_pre, w_first).astype(bf16)
    sent_back = gather_back(grad_input)
    grad_w1 = transpose_dot(flat_in, grad_pre).astype(bf16)
    grad_w1 = lax.all_to_all(grad_w1, "dp", split_axis=0, concat_axis=1, tiled=True)
    grad_b1 = jnp.sum(grad_pre, axis=0, dtype=f32)[None]
    grad_w2 = transpose_dot(activated, flat_grad)[None]
    grad_b2 = jnp.sum(flat_grad, axis=0, dtype=f32)
    grad_b2 = lax.dynamic_slice(grad_b2, (dp_index * owned,), (owned,))[None]

    chosen_one = jnp.dot(hot_one, returned, preferred_element_type=f32)
    chosen_two = jnp.dot(hot_two, returned, preferred_element_type=f32)
    final_rows = after_attn + (gate_one[:, None] * chosen_one + gate_two[:, None] * chosen_two)
    mixed_out = final_rows.astype(bf16).reshape(tokens.shape)
    grad_out = jnp.where(live_rows[:, None], cot_rows.astype(f32), 0.0)
    grad_gate_one = jnp.sum(grad_out * chosen_one, axis=-1, keepdims=True)
    grad_gate_two = jnp.sum(grad_out * chosen_two, axis=-1, keepdims=True)
    grad_probs = jnp.where(pair_hot[:, 0], grad_gate_one, 0.0) + jnp.where(
        pair_hot[:, 1], grad_gate_two, 0.0
    )
    grad_logits = router_probs * (
        grad_probs - jnp.sum(router_probs * grad_probs, axis=-1, keepdims=True)
    )
    grad_logits = grad_logits.astype(bf16)
    grad_router = transpose_dot(normed_two, grad_logits)
    grad_normed = jnp.dot(hot_both, sent_back, preferred_element_type=f32)
    grad_normed = grad_normed + dot_transpose(grad_logits, router_full)
    grad_gain_two = jnp.sum(grad_normed * normal_two, axis=0)
    grad_shift_two = jnp.sum(grad_normed, axis=0)
    grad_after = grad_out + norm_back(grad_normed, normal_two, inverse_two, gain_two)
    grad_out_shift = jnp.sum(grad_after, axis=0)
    grad_branch = grad_after.astype(bf16)
    grad_attended = (
        dot_transpose(grad_branch, out_full)
        .astype(bf16)
        .reshape(img_count, seq_len, head_count, head_size)
    )
    grad_weights = jnp.einsum(
        "isha,itha->ihst", grad_attended, value_vecs, preferred_element_type=f32
    )
    row_dot = jnp.sum(prob_attn * grad_weights, axis=-1, keepdims=True)
    grad_scores = jnp.where(key_live, prob_attn * (grad_weights - row_dot), 0.0).astype(bf16)
    grad_queries = (
        jnp.einsum("ihst,itha->isha", grad_scores, key_vecs, preferred_element_type=f32)
        * scale_factor
    )
    grad_keys = (
        jnp.einsum("ihst,isha->itha", grad_scores, queries, preferred_element_type=f32)
        * scale_factor
    )
    grad_values = jnp.einsum("ihst,isha->itha", weights, grad_attended, preferred_element_type=f32)
    grad_projected = (
        jnp.stack([grad_queries, grad_keys, grad_values], axis=2)
        .reshape(tok_rows, 3 * model_width)
        .astype(bf16)
    )
    grad_projected, grad_w1 = lax.optimization_barrier((grad_projected, grad_w1))
    grad_w1 = grad_w1.astype(f32)[None]
    column_sums = jnp.sum(grad_projected, axis=0, dtype=f32)
    grad_qv = jnp.concatenate([column_sums[:model_width], column_sums[2 * model_width :]])
    grad_normed_one = dot_transpose(grad_projected, qkv_full)
    grad_gain_one = jnp.sum(grad_normed_one * normal_one, axis=0)
    grad_shift_one = jnp.sum(grad_normed_one, axis=0)
    grad_inputs = grad_after + norm_back(grad_normed_one, normal_one, inverse_one, gain_one)
    tokens_grad = grad_inputs.astype(bf16).reshape(tokens.shape)

    small_grads = (
        grad_gain_one,
        grad_shift_one,
        grad_qv,
        grad_out_shift,
        grad_gain_two,
        grad_shift_two,
        grad_router,
    )
    small_pack = jnp.concatenate([part.reshape(dp_count, -1) for part in small_grads], axis=1)
    qkv_part = 3 * model_width // expert_count
    out_part = model_width // expert_count
    share = qkv_part + out_part
    extra = -(-small_pack.shape[1] // (expert_count * share))
    small_pack = jnp.pad(
        small_pack, ((0, 0), (0, expert_count * share * extra - small_pack.shape[1]))
    )
    small_pack = (
        small_pack.astype(bf16)
        .reshape(dp_count, expert_count, extra, share)
        .transpose(1, 0, 2, 3)
        .reshape(expert_count, dp_count * extra, share)
    )
    column_share = jnp.concatenate(
        [
            grad_projected.reshape(tok_rows, expert_count, qkv_part),
            grad_branch.reshape(tok_rows, expert_count, out_part),
        ],
        axis=2,
    ).transpose(1, 0, 2)
    shares_in = lax.all_to_all(
        jnp.concatenate([column_share, small_pack], axis=1),
        "expert",
        split_axis=0,
        concat_axis=0,
        tiled=True,
    )
    token_share = shares_in[:, :tok_rows].reshape(expert_count * tok_rows, share)
    small_share = jnp.sum(shares_in[:, tok_rows:].astype(f32), axis=0)
    qkv_rows = transpose_dot(in_gather[:, :model_width], token_share[:, :qkv_part])
    out_rows = transpose_dot(in_gather[:, model_width:], token_share[:, qkv_part:])
    partial_grad = jnp.concatenate(
        [
            jnp.concatenate([qkv_rows, out_rows], axis=1).reshape(dp_count, owned, share),
            small_share.reshape(dp_count, extra, share),
        ],
        axis=1,
    ).astype(bf16)
    summed = lax.all_to_all(partial_grad, "dp", split_axis=0, concat_axis=0, tiled=True)
    summed = jnp.sum(summed.astype(f32), axis=0).astype(bf16)
    everyone = lax.all_to_all(
        jnp.broadcast_to(summed[None], (expert_count,) + summed.shape),
        "expert",
        split_axis=0,
        concat_axis=0,
        tiled=True,
    ).astype(f32)
    qkv_total = everyone[:, :owned, :qkv_part].transpose(1, 0, 2).reshape(owned, 3 * model_width)
    out_total = everyone[:, :owned, qkv_part:].transpose(1, 0, 2).reshape(owned, model_width)
    small_total = everyone[:, owned:].reshape(-1)
    (
        gain_one_total,
        shift_one_total,
        qv_total,
        out_shift_total,
        gain_two_total,
        shift_two_total,
        router_total,
    ) = (
        small_total[cuts[i] : cuts[i + 1]].reshape(small_in[i].shape) for i in range(7)
    )
    return (
        mixed_out,
        tokens_grad,
        gain_one_total,
        shift_one_total,
        qkv_total,
        qv_total,
        out_total,
        out_shift_total,
        gain_two_total,
        shift_two_total,
        router_total,
        grad_w1,
        grad_b1,
        grad_w2,
        grad_b2,
    )


def solution(mesh):
    in_specs = (
        P(("expert", "dp"), None, None),
        P(("expert", "dp"), None, None),
        P(("expert", "dp")),
        P(("expert", "dp"), None, None),
        P("dp"),
        P("dp"),
        P("dp", None),
        P("dp"),
        P("dp", None),
        P("dp"),
        P("dp"),
        P("dp"),
        P("dp", None),
        P("expert", "dp", None),
        P("expert", "dp"),
        P("expert", "dp", None),
        P("expert", "dp"),
    )
    out_specs = (
        P(("expert", "dp"), None, None),
        P(("expert", "dp"), None, None),
        P("dp"),
        P("dp"),
        P("dp", None),
        P("dp"),
        P("dp", None),
        P("dp"),
        P("dp"),
        P("dp"),
        P("dp", None),
        P("expert", "dp", None),
        P("expert", "dp"),
        P("expert", "dp", None),
        P("expert", "dp"),
    )
    return jax.shard_map(shards, mesh=mesh, in_specs=in_specs, out_specs=out_specs, check_vma=False)
```
